256 devices in a mesh: replica: 32 (over y, z_hi, core), fsdp: 2 (over z_lo), tensor: 4 (over x).
Axes of the slice: x: 4, y: 4, z: 8 (z_hi: 4, z_lo: 2; z = z_hi * 2 + z_lo), core: 2. Of those that a mesh axis runs over, the one named last changes fastest.
Arguments:
- anchor: float32 [256, 28672], P('fsdp', 'tensor')
- local_weights: float32 [32, 256, 28672], P('replica', 'fsdp', 'tensor')
- momentum: float32 [256, 4, 7168], P('fsdp', 'tensor', 'replica'), may hold values from -3 to 3
Outputs:
- new_anchor: float32 [256, 28672], P('fsdp', 'tensor')
- new_momentum: float32 [256, 4, 7168], P('fsdp', 'tensor', 'replica')
The draws below stay inside these ranges and needn't reach their ends.
All inputs are finite; a program needn't handle non-finite values.
Results may differ from the reference program's by a relative error of at most 0.00013.
Values sent between devices are 32-bit elements; how exact they have to be, the bound alone decides.
No kernel may reach another device: no remote copies, remote signals or barrier semaphores. Data moves between devices by JAX's collectives and lax.ppermute only.
A program may use at most 64 MiB of HBM per device.

```python
import math
import jax
import jax.numpy as jnp
from jax import lax

FF = 28672
ROWS = 256
REPLICAS = 32
SPLITS = 4
COLS_T = 7168


def base_values(key):
    return jnp.clip(jax.random.normal(key, (ROWS, FF), jnp.float32), -5.0, 5.0)


def draw_anchor(key, part):
    return base_values(key)


def draw_local_weights(key, part):
    shared = base_values(key)
    key = jax.random.fold_in(key, 11)
    key_own = jax.random.fold_in(key, 1)
    key_rough = jax.random.fold_in(key, 2)
    row_pos = jnp.arange(ROWS, dtype=jnp.float32) / ROWS
    col_pos = jnp.arange(FF, dtype=jnp.float32) / FF
    scaling = jnp.power(10.0, row_pos)[:, None] * jnp.power(10.0, col_pos)[None, :]
    rough = jax.random.uniform(key_rough, (REPLICAS, ROWS, FF), jnp.float32, 0.5, 1.5)
    own_part = jax.random.normal(key_own, (REPLICAS, ROWS, FF), jnp.float32)
    drift = 0.2 * scaling[None] * own_part * rough
    return shared[None] - drift


def levels(rng, dims, split, low, high):
    loudness = 1.0
    for axis_at, parts in split:
        heights = jax.random.uniform(jax.random.fold_in(jax.random.fold_in(rng, 6), axis_at), (parts,), jnp.float32, low / len(split), high / len(split))
        loudness = loudness * jnp.repeat(jnp.exp(heights), dims[axis_at] // parts).reshape((-1,) + (1,) * (len(dims) - 1 - axis_at))
    return loudness


def centred(key, shape, spread, bound, pieces=(), held_as=jnp.bfloat16):
    factor_of = levels(key, shape, pieces, -0.22, 0.18) if pieces else 1.0
    entries = jax.random.normal(key, shape, jnp.float32) * spread * factor_of
    return jnp.minimum(jnp.maximum(entries, -bound), bound).astype(held_as)


def setup_inputs(seed: int = 0) -> dict:
    keys = jax.random.split(jax.random.key(seed), 4)
    return {
        "anchor": draw_anchor(jax.random.fold_in(keys[3], 71), 0),
        "local_weights": draw_local_weights(jax.random.fold_in(keys[3], 71), 0),
        "momentum": centred(keys[2], (ROWS, SPLITS, COLS_T), 0.5, 3.0, ((0, 2), (1, 4), (2, 32)), jnp.float32),
    }


momentum_decay = 0.9
outer_rate = 0.7
clip_rms = 0.25

def reference(anchor, local_weights, momentum):

    def add_replica(index, summed):
        replica_weights = lax.dynamic_index_in_dim(local_weights, index, 0, keepdims=False)
        return summed + (anchor - replica_weights)
    summed = lax.fori_loop(0, REPLICAS, add_replica, jnp.zeros((ROWS, FF), jnp.float32))
    pseudo_grad = summed / REPLICAS
    grad_norm = jnp.sqrt(jnp.sum(pseudo_grad * pseudo_grad))
    ceiling = clip_rms * math.sqrt(ROWS * FF)
    clipped = pseudo_grad * (ceiling / jnp.maximum(grad_norm, ceiling))
    moment_whole = momentum.reshape(ROWS, FF)
    new_momentum = momentum_decay * moment_whole + clipped
    update = clipped + momentum_decay * new_momentum
    new_anchor = anchor - outer_rate * update
    return (new_anchor, new_momentum.reshape(ROWS, SPLITS, COLS_T))
```

```python
import math

import jax
import jax.numpy as jnp
from jax import lax
from jax.sharding import Mesh, PartitionSpec as P

momentum_decay = 0.9
outer_rate = 0.7
clip_rms = 0.25

REPLICA = ("y", "zh", "core")
SUB = 8
LANE = 128


def swap(x, axis, mask):
    n = lax.axis_size(axis)
    return lax.ppermute(x, axis, [(i, i ^ mask) for i in range(n)])


def shift(x, axis, by):
    n = lax.axis_size(axis)
    return lax.ppermute(x, axis, [(i, (i + by) % n) for i in range(n)])


def tiles(x):
    rows, cols = x.shape
    return x.reshape(rows // SUB, SUB, cols // LANE, LANE).transpose(0, 2, 1, 3)


def untiles(x):
    blocks, lanes = x.shape[:2]
    return x.transpose(0, 2, 1, 3).reshape(blocks * SUB, lanes * LANE)


def gather4(x, axis):
    me = lax.axis_index(axis)
    parts = [(0, x)] + [(by, shift(x, axis, by)) for by in (1, 3, 2)]
    whole = jnp.zeros((4,) + x.shape, x.dtype)
    for by, part in parts:
        whole = lax.dynamic_update_index_in_dim(whole, part, (me - by) % 4, 0)
    return whole


def on_device(anchor, local_weights, momentum):
    y, zh, core = (lax.axis_index(a) for a in REPLICA)
    replicas = math.prod(lax.axis_size(a) for a in REPLICA)
    elements = anchor.shape[0] * anchor.shape[1] * lax.axis_size("zl") * lax.axis_size("x")
    ceiling = clip_rms * math.sqrt(elements)

    a_tiles, l_tiles = tiles(anchor), tiles(local_weights[0])
    blocks, lanes = a_tiles.shape[:2]
    quarter = lanes // 4

    gray_y, gray_z = (y ^ (y >> 1)) & 1, (zh ^ (zh >> 1)) & 1
    streams = (
        (("y", 1, gray_y), ("y", 3, y >> 1), ("zh", 1, gray_z), ("zh", 3, zh >> 1)),
        (("y", 3, y >> 1), ("y", 1, y & 1), ("zh", 3, zh >> 1), ("zh", 1, zh & 1)),
    )

    def drift(stream, of_core, row, count):
        at = (row, (2 * stream + of_core) * quarter, 0, 0)
        size = (count, quarter, SUB, LANE)
        return lax.dynamic_slice(a_tiles, at, size) - lax.dynamic_slice(l_tiles, at, size)

    received = [[(0, swap(drift(s, 1 - core, 0, blocks), "core", 1))] for s in (0, 1)]
    first = [0, 0]
    count = blocks

    def total(s, row, n):
        value = drift(s, core, row, n)
        for origin, part in received[s]:
            value = value + lax.dynamic_slice_in_dim(part, row - origin, n, 0)
        return value

    for step in range(4):
        count //= 2
        for s in (0, 1):
            axis, mask, bit = streams[s][step]
            sent = total(s, first[s] + (1 - bit) * count, count)
            first[s] = first[s] + bit * count
            received[s].append((first[s], swap(sent, axis, mask)))
    own = [total(s, first[s], count) * (1.0 / replicas) for s in (0, 1)]

    squares = sum(jnp.sum(p * p, axis=(0, 1)) for p in own)
    for axis, mask in (("x", 1), ("x", 2), ("zl", 1), ("core", 1), ("y", 1), ("zh", 1), ("y", 3), ("zh", 3)):
        squares = squares + swap(squares, axis, mask)
    norm = jnp.sqrt(jnp.sum(squares))
    scaling = ceiling / jnp.maximum(norm, ceiling)

    own_moment = momentum[:, 0, :].T
    shard = own_moment.shape[0]
    gathered = own_moment.reshape(shard // SUB, SUB, LANE)
    gathered = gather4(gathered, "zh")
    gathered = gather4(gathered, "y")
    other = swap(gathered, "core", 1)
    moment = jnp.stack([jnp.where(core == 0, gathered, other), jnp.where(core == 0, other, gathered)], 2)
    moment = tiles(moment.reshape(replicas * shard, LANE).T)
    rest = a_tiles - outer_rate * momentum_decay * momentum_decay * moment

    for step in (3, 2, 1, 0):
        for s in (0, 1):
            axis, mask, bit = streams[s][step]
            other = swap(own[s], axis, mask)
            low, high = jnp.where(bit == 0, own[s], other), jnp.where(bit == 0, other, own[s])
            own[s] = jnp.concatenate([low, high], 0)
    pieces = []
    for s in (0, 1):
        other = swap(own[s], "core", 1)
        pieces += [jnp.where(core == 0, own[s], other), jnp.where(core == 0, other, own[s])]
    pseudo_grad = jnp.concatenate(pieces, 1)

    new_anchor = rest - (outer_rate * (1.0 + momentum_decay)) * scaling * pseudo_grad

    at = (y * 8 + zh * 2 + core) * shard
    tile_at = jnp.minimum(at // LANE, lanes - 3)
    cols = lax.dynamic_slice_in_dim(pseudo_grad, tile_at, 3, 1)
    cols = cols.transpose(1, 3, 0, 2).reshape(3 * LANE // SUB, SUB, LANE)
    cols = lax.dynamic_slice_in_dim(cols, (at - tile_at * LANE) // SUB, shard // SUB, 0)
    new_moment = momentum_decay * own_moment + scaling * cols.reshape(shard, LANE)
    return untiles(new_anchor), new_moment.T[:, None, :]


def solution(mesh):
    fine = Mesh(mesh.devices.reshape(4, 4, 2, 2, 4), ("y", "zh", "core", "zl", "x"))
    in_specs = (P("zl", "x"), P(REPLICA, "zl", "x"), P("zl", "x", REPLICA))
    out_specs = (P("zl", "x"), P("zl", "x", REPLICA))
    return jax.shard_map(on_device, mesh=fine, in_specs=in_specs, out_specs=out_specs, check_vma=False)
```

```python
import math

import jax
import jax.numpy as jnp
from jax import lax
from jax.experimental import pallas as pl
from jax.experimental.pallas import tpu as pltpu
from jax.sharding import Mesh, PartitionSpec as P

momentum_decay = 0.9
outer_rate = 0.7
clip_rms = 0.25

REPLICA = ("y", "zh", "core")
SUB = 8
LANE = 128


def swap(x, axis, mask):
    n = lax.axis_size(axis)
    return lax.ppermute(x, axis, [(i, i ^ mask) for i in range(n)])


def after(x, *others):
    return lax.optimization_barrier((x,) + others)[0]


def rows_at(x, start, count):
    return lax.dynamic_slice_in_dim(x, start, count, 0)


def half(x, bit):
    middle = x.shape[-1] // 2
    return jnp.where(bit == 0, x[..., :middle], x[..., middle:])


def join(mine, other, bit, dim):
    low, high = jnp.where(bit == 0, mine, other), jnp.where(bit == 0, other, mine)
    return jnp.concatenate([low, high], dim)


def rest_kernel(core_ref, anchor_ref, mine_ref, other_ref, rest_ref):
    groups, shard, lanes = mine_ref.shape
    swapped = core_ref[0] != 0
    parts = []
    for g in range(groups):
        mine, other = mine_ref[g], other_ref[g]
        parts += [jnp.where(swapped, other, mine), jnp.where(swapped, mine, other)]
    moment = jnp.concatenate(parts, 0).T
    rest_ref[...] = anchor_ref[...] - (outer_rate * momentum_decay * momentum_decay) * moment


def rest_of(core, anchor, mine, other):
    rows, cols = anchor.shape
    groups, shard, _ = mine.shape
    per = 2
    width = per * 2 * shard
    part = pl.BlockSpec((per, shard, rows), lambda i, c: (i, 0, 0))
    whole = pl.BlockSpec((rows, width), lambda i, c: (0, i))
    return pl.pallas_call(
        rest_kernel,
        out_shape=jax.ShapeDtypeStruct(anchor.shape, anchor.dtype),
        grid_spec=pltpu.PrefetchScalarGridSpec(
            num_scalar_prefetch=1, grid=(groups // per,), in_specs=[whole, part, part], out_specs=whole
        ),
        cost_estimate=pl.CostEstimate(flops=2 * rows * cols, bytes_accessed=12 * rows * cols, transcendentals=0),
        name="rest",
    )(core.reshape(1), anchor, mine, other)


def on_device(anchor, local_weights, momentum):
    y, zh, core = (lax.axis_index(a) for a in REPLICA)
    replicas = math.prod(lax.axis_size(a) for a in REPLICA)
    elements = anchor.shape[0] * anchor.shape[1] * lax.axis_size("zl") * lax.axis_size("x")
    ceiling = clip_rms * math.sqrt(elements)
    rows, cols = anchor.shape
    blocks = rows // SUB
    a_rows = anchor.reshape(blocks, SUB, cols)
    l_rows = local_weights.reshape(blocks, SUB, cols)

    gray_y, gray_z = (y ^ (y >> 1)) & 1, (zh ^ (zh >> 1)) & 1
    over_y = ((("y", 1, gray_y), ("y", 3, y >> 1)), (("y", 3, y >> 1), ("y", 1, y & 1)))
    over_z = ((("zh", 1, gray_z), ("zh", 3, zh >> 1)), (("zh", 3, zh >> 1), ("zh", 1, zh & 1)))
    each = blocks // 2
    streams = (0, 1)
    count = each // 2
    got = [[], []]
    first = [s * each + core * count for s in streams]

    def total(s, start, n, locals_=l_rows):
        value = rows_at(a_rows, start, n) - rows_at(locals_, start, n)
        for origin, part in got[s]:
            value = value + rows_at(part, start - origin, n)
        return value

    def hold(s, *others):
        origin, part = got[s][-1]
        got[s][-1] = (origin, after(part, *others))

    own_moment = momentum[:, 0, :].T
    shard = own_moment.shape[0]

    sent = [total(0, (1 - core) * count, count)]
    sent.append(total(1, each + (1 - core) * count, count, after(l_rows, sent[0])))
    for s in streams:
        got[s].append((first[s], swap(sent[s], "core", 1)))
    moment_z = after(own_moment, sent[1])
    beside = [swap(moment_z, "zh", 1), swap(moment_z, "zh", 3)]

    for step in (0, 1):
        count //= 2
        sent = []
        for s in streams:
            axis, mask, bit = over_y[s][step]
            if s == 1:
                hold(1, sent[0])
            elif step == 1:
                hold(0, *beside)
            sent.append(total(s, first[s] + (1 - bit) * count, count))
            first[s] = first[s] + bit * count
        for s in streams:
            axis, mask, bit = over_y[s][step]
            got[s].append((first[s], swap(sent[s], axis, mask)))
        if step == 1:
            third = swap(after(moment_z, sent[1]), "zh", 2)
    whole = jnp.zeros((4, shard, LANE), own_moment.dtype)
    for mask, part in ((0, own_moment), (1, beside[0]), (3, beside[1]), (2, third)):
        whole = lax.dynamic_update_index_in_dim(whole, part, zh ^ mask, 0)

    hold(0, whole)
    own = [total(0, first[0], count)]
    hold(1, own[0])
    own.append(total(1, first[1], count))
    for step in (0, 1):
        sent = []
        for s in streams:
            axis, mask, bit = over_z[s][step]
            if s == 1:
                own[1] = after(own[1], sent[0])
            sent.append(half(own[s], 1 - bit))
        if step == 0:
            moment_y = after(whole, sent[1])
            beside = [swap(moment_y, "y", 1), swap(moment_y, "y", 3)]
        for s in streams:
            axis, mask, bit = over_z[s][step]
            own[s] = half(own[s], bit) + swap(sent[s], axis, mask)
    own = [p * (1.0 / replicas) for p in own]
    own[0] = after(own[0], *beside)
    own[1] = after(own[1], own[0])

    squares = sum(jnp.sum(p.reshape(SUB, -1, LANE) ** 2, axis=1) for p in own)

    def add_squares(squares, *steps):
        for axis, mask in steps:
            squares = squares + swap(squares, axis, mask)
        return squares

    squares = add_squares(after(squares, own[1]), ("x", 1))
    third = swap(after(moment_y, own[1]), "y", 2)
    for step in (1, 0):
        if step == 0:
            own[0] = after(own[0], squares)
            own[1] = after(own[1], own[0])
            squares = add_squares(after(squares, own[1]), ("x", 2))
        for s in streams:
            axis, mask, bit = over_z[s][step]
            own[s] = join(own[s], swap(own[s], axis, mask), bit, 2)
    whole = jnp.zeros((4, 4, shard, LANE), own_moment.dtype)
    for mask, part in ((0, moment_y), (1, beside[0]), (3, beside[1]), (2, third)):
        whole = lax.dynamic_update_index_in_dim(whole, part, y ^ mask, 0)
    whole = whole.reshape(16, shard, LANE)

    own[0] = after(own[0], squares, whole)
    own[1] = after(own[1], own[0])
    squares = add_squares(after(squares, own[1]), ("zl", 1), ("core", 1))
    whole = after(whole, own[1])
    other = swap(whole, "core", 1)
    for s in streams:
        axis, mask, bit = over_y[s][1]
        own[s] = join(own[s], swap(own[s], axis, mask), bit, 0)
    own[0] = after(own[0], squares, other)
    own[1] = after(own[1], own[0])
    squares = add_squares(after(squares, own[1]), ("zh", 1), ("zh", 3), ("y", 1))
    rest = rest_of(core, anchor, after(whole, own[1]), other)
    for s in streams:
        axis, mask, bit = over_y[s][0]
        own[s] = join(own[s], swap(own[s], axis, mask), bit, 0)

    own[0] = after(own[0], squares, rest)
    own[1] = after(own[1], own[0])
    squares = add_squares(after(squares, own[1]), ("y", 3))
    others = [swap(own[s], "core", 1) for s in streams]
    norm = jnp.sqrt(jnp.sum(squares))
    scaling = ceiling / jnp.maximum(norm, ceiling)

    factor = (outer_rate * (1.0 + momentum_decay)) * scaling
    at = (y * 8 + zh * 2 + core) * shard
    count = each // 2
    result = rest.reshape(blocks, SUB, cols)
    for pieces, of_core in ((own, core), (others, 1 - core)):
        for s in streams:
            start = s * each + of_core * count
            value = rows_at(result, start, count) - factor * pieces[s]
            result = lax.dynamic_update_slice_in_dim(result, value, start, 0)

    columns = []
    for s in streams:
        mine, other = (lax.dynamic_slice_in_dim(p[s].reshape(count * SUB, cols), at, shard, 1) for p in (own, others))
        columns.append(join(mine, other, core, 0))
    columns = jnp.concatenate(columns, 0)
    new_moment = momentum_decay * momentum[:, 0, :] + scaling * columns
    return result.reshape(rows, cols), new_moment[:, None, :]


def solution(mesh):
    fine = Mesh(mesh.devices.reshape(4, 4, 2, 2, 4), ("y", "zh", "core", "zl", "x"))
    in_specs = (P("zl", "x"), P(REPLICA, "zl", "x"), P("zl", "x", REPLICA))
    out_specs = (P("zl", "x"), P("zl", "x", REPLICA))
    return jax.shard_map(on_device, mesh=fine, in_specs=in_specs, out_specs=out_specs, check_vma=False)
```

```python
import math

import jax
import jax.numpy as jnp
from jax import lax
from jax.experimental import pallas as pl
from jax.experimental.pallas import tpu as pltpu
from jax.sharding import Mesh, PartitionSpec as P

momentum_decay = 0.9
outer_rate = 0.7
clip_rms = 0.25

REPLICA = ("y", "zh", "core")
SUB = 8
LANE = 128


def swap(x, axis, mask):
    n = lax.axis_size(axis)
    return lax.ppermute(x, axis, [(i, i ^ mask) for i in range(n)])


def swap_all(x, masks):
    axes = tuple(masks)
    sizes = [lax.axis_size(a) for a in axes]
    mask = 0
    for a, n in zip(axes, sizes):
        mask = mask * n + masks[a]
    return lax.ppermute(x, axes, [(i, i ^ mask) for i in range(math.prod(sizes))])


def after(x, *others):
    return lax.optimization_barrier((x,) + others)[0]


def rows_at(x, start, count):
    return lax.dynamic_slice_in_dim(x, start, count, 0)


def half(x, bit):
    middle = x.shape[-1] // 2
    return jnp.where(bit == 0, x[..., :middle], x[..., middle:])


def join(mine, other, bit, dim):
    low, high = jnp.where(bit == 0, mine, other), jnp.where(bit == 0, other, mine)
    return jnp.concatenate([low, high], dim)


def rest_kernel(core_ref, anchor_ref, mine_ref, other_ref, rest_ref):
    groups, shard, lanes = mine_ref.shape
    swapped = core_ref[0] != 0
    parts = []
    for g in range(groups):
        mine, other = mine_ref[g], other_ref[g]
        parts += [jnp.where(swapped, other, mine), jnp.where(swapped, mine, other)]
    moment = jnp.concatenate(parts, 0).T
    rest_ref[...] = anchor_ref[...] - (outer_rate * momentum_decay * momentum_decay) * moment


def rest_of(core, anchor, mine, other):
    rows, cols = anchor.shape
    groups, shard, _ = mine.shape
    per = 2
    width = per * 2 * shard
    part = pl.BlockSpec((per, shard, rows), lambda i, c: (i, 0, 0))
    whole = pl.BlockSpec((rows, width), lambda i, c: (0, i))
    return pl.pallas_call(
        rest_kernel,
        out_shape=jax.ShapeDtypeStruct(anchor.shape, anchor.dtype),
        grid_spec=pltpu.PrefetchScalarGridSpec(
            num_scalar_prefetch=1, grid=(groups // per,), in_specs=[whole, part, part], out_specs=whole
        ),
        cost_estimate=pl.CostEstimate(flops=2 * rows * cols, bytes_accessed=12 * rows * cols, transcendentals=0),
        name="rest",
    )(core.reshape(1), anchor, mine, other)


def on_device(anchor, local_weights, momentum):
    y, zh, core = (lax.axis_index(a) for a in REPLICA)
    replicas = math.prod(lax.axis_size(a) for a in REPLICA)
    elements = anchor.shape[0] * anchor.shape[1] * lax.axis_size("zl") * lax.axis_size("x")
    ceiling = clip_rms * math.sqrt(elements)
    rows, cols = anchor.shape
    blocks = rows // SUB
    a_rows = anchor.reshape(blocks, SUB, cols)
    l_rows = local_weights.reshape(blocks, SUB, cols)

    gray_y, gray_z = (y ^ (y >> 1)) & 1, (zh ^ (zh >> 1)) & 1
    over_y = ((("y", 1, gray_y), ("y", 3, y >> 1)), (("y", 3, y >> 1), ("y", 1, y & 1)))
    over_z = ((("zh", 1, gray_z), ("zh", 3, zh >> 1)), (("zh", 3, zh >> 1), ("zh", 1, zh & 1)))
    each = blocks // 2
    streams = (0, 1)
    count = each // 2
    got = [[], []]
    first = [s * each + core * count for s in streams]

    def total(s, start, n, locals_=l_rows):
        value = rows_at(a_rows, start, n) - rows_at(locals_, start, n)
        for origin, part in got[s]:
            value = value + rows_at(part, start - origin, n)
        return value

    def hold(s, *others):
        origin, part = got[s][-1]
        got[s][-1] = (origin, after(part, *others))

    own_moment = momentum[:, 0, :].T
    shard = own_moment.shape[0]

    sent = [total(0, (1 - core) * count, count)]
    sent.append(total(1, each + (1 - core) * count, count, after(l_rows, sent[0])))
    for s in streams:
        got[s].append((first[s], swap(sent[s], "core", 1)))

    for step in (0, 1):
        count //= 2
        sent = []
        for s in streams:
            axis, mask, bit = over_y[s][step]
            if s == 1:
                hold(1, sent[0])
            elif step == 1:
                hold(0, *beside)
            sent.append(total(s, first[s] + (1 - bit) * count, count))
            first[s] = first[s] + bit * count
        for s in streams:
            axis, mask, bit = over_y[s][step]
            got[s].append((first[s], swap(sent[s], axis, mask)))
        moment_z = after(own_moment, sent[1])
        if step == 0:
            beside = [swap(moment_z, "zh", 1), swap(moment_z, "zh", 3)]
        else:
            third = swap(moment_z, "zh", 2)
    whole = jnp.zeros((4, shard, LANE), own_moment.dtype)
    for mask, part in ((0, own_moment), (1, beside[0]), (3, beside[1]), (2, third)):
        whole = lax.dynamic_update_index_in_dim(whole, part, zh ^ mask, 0)

    hold(0, whole)
    own = [total(0, first[0], count)]
    hold(1, own[0])
    own.append(total(1, first[1], count))
    for step in (0, 1):
        sent = []
        for s in streams:
            axis, mask, bit = over_z[s][step]
            if s == 1:
                own[1] = after(own[1], sent[0])
            sent.append(half(own[s], 1 - bit))
        if step == 0:
            moment_y = after(whole, sent[1])
            beside = [swap(moment_y, "y", 1), swap(moment_y, "y", 3)]
        for s in streams:
            axis, mask, bit = over_z[s][step]
            own[s] = half(own[s], bit) + swap(sent[s], axis, mask)
    own = [p * (1.0 / replicas) for p in own]
    own[0] = after(own[0], *beside)
    own[1] = after(own[1], own[0])

    squares = sum(jnp.sum(p.reshape(SUB, -1, LANE) ** 2, axis=1) for p in own)

    def add_squares(squares, *steps):
        return squares + sum(swap_all(squares, masks) for masks in steps)

    squares = add_squares(after(squares, own[1]), {"x": 1}, {"x": 2}, {"x": 3})
    third = swap(after(moment_y, own[1]), "y", 2)
    for step in (1, 0):
        if step == 0:
            own[0] = after(own[0], squares)
            own[1] = after(own[1], own[0])
            squares = add_squares(after(squares, own[1]), {"core": 1}, {"zl": 1}, {"core": 1, "zl": 1})
        for s in streams:
            axis, mask, bit = over_z[s][step]
            own[s] = join(own[s], swap(own[s], axis, mask), bit, 2)
    whole = jnp.zeros((4, 4, shard, LANE), own_moment.dtype)
    for mask, part in ((0, moment_y), (1, beside[0]), (3, beside[1]), (2, third)):
        whole = lax.dynamic_update_index_in_dim(whole, part, y ^ mask, 0)
    whole = whole.reshape(16, shard, LANE)

    own[0] = after(own[0], squares, whole)
    own[1] = after(own[1], own[0])
    squares = add_squares(after(squares, own[1]), {"y": 1}, {"y": 2}, {"y": 3})
    whole = after(whole, own[1])
    other = swap(whole, "core", 1)
    for s in streams:
        axis, mask, bit = over_y[s][1]
        own[s] = join(own[s], swap(own[s], axis, mask), bit, 0)
    own[0] = after(own[0], squares, other)
    own[1] = after(own[1], own[0])
    squares = add_squares(after(squares, own[1]), {"zh": 1}, {"zh": 2}, {"zh": 3})
    rest = rest_of(core, anchor, after(whole, own[1]), other)
    for s in streams:
        axis, mask, bit = over_y[s][0]
        own[s] = join(own[s], swap(own[s], axis, mask), bit, 0)

    own[0] = after(own[0], squares, rest)
    own[1] = after(own[1], own[0])
    others = [swap(own[s], "core", 1) for s in streams]
    norm = jnp.sqrt(jnp.sum(squares))
    scaling = ceiling / jnp.maximum(norm, ceiling)

    factor = (outer_rate * (1.0 + momentum_decay)) * scaling
    at = (y * 8 + zh * 2 + core) * shard
    count = each // 2
    result = rest.reshape(blocks, SUB, cols)
    for pieces, of_core in ((own, core), (others, 1 - core)):
        for s in streams:
            start = s * each + of_core * count
            value = rows_at(result, start, count) - factor * pieces[s]
            result = lax.dynamic_update_slice_in_dim(result, value, start, 0)

    columns = []
    for s in streams:
        mine, other = (lax.dynamic_slice_in_dim(p[s].reshape(count * SUB, cols), at, shard, 1) for p in (own, others))
        columns.append(join(mine, other, core, 0))
    columns = jnp.concatenate(columns, 0)
    new_moment = momentum_decay * momentum[:, 0, :] + scaling * columns
    return result.reshape(rows, cols), new_moment[:, None, :]


def solution(mesh):
    fine = Mesh(mesh.devices.reshape(4, 4, 2, 2, 4), ("y", "zh", "core", "zl", "x"))
    in_specs = (P("zl", "x"), P(REPLICA, "zl", "x"), P("zl", "x", REPLICA))
    out_specs = (P("zl", "x"), P("zl", "x", REPLICA))
    return jax.shard_map(on_device, mesh=fine, in_specs=in_specs, out_specs=out_specs, check_vma=False)
```

```python
import math

import jax
import jax.numpy as jnp
from jax import lax
from jax.experimental import pallas as pl
from jax.experimental.pallas import tpu as pltpu
from jax.sharding import Mesh, PartitionSpec as P

momentum_decay = 0.9
outer_rate = 0.7
clip_rms = 0.25

REPLICA = ("y", "zh", "core")
SUB = 8
LANE = 128
MASKS = (1, 3, 2)
HOLD_BYTES = 2 << 20
IN_VMEM = pl.BlockSpec(memory_space=pltpu.VMEM)


def swap(x, /, **masks):
    axes = tuple(masks)
    sizes = [lax.axis_size(a) for a in axes]
    mask = 0
    for a, n in zip(axes, sizes):
        mask = mask * n + masks[a]
    return lax.ppermute(x, axes, [(i, i ^ mask) for i in range(math.prod(sizes))])


def after(x, other):
    tile = other.reshape(-1, SUB, other.shape[-1])[0, :, :LANE]
    return x + 0.0 * jnp.clip(tile, -1.0, 1.0)


def hold_kernel(tile_ref, x_ref, out_ref):
    del tile_ref
    out_ref[...] = x_ref[...]


def hold(x, other):
    tile = other.reshape(-1, SUB, other.shape[-1])[0, :, :LANE]
    flat = x.reshape(-1, LANE)
    return pl.pallas_call(
        hold_kernel,
        out_shape=jax.ShapeDtypeStruct(flat.shape, flat.dtype),
        in_specs=[IN_VMEM, IN_VMEM],
        out_specs=IN_VMEM,
        cost_estimate=pl.CostEstimate(flops=0, bytes_accessed=HOLD_BYTES, transcendentals=0),
        compiler_params=pltpu.CompilerParams(vmem_limit_bytes=16 << 20),
        name="hold",
    )(tile, flat).reshape(x.shape)


def rows_at(x, start, count):
    return lax.dynamic_slice_in_dim(x, start, count, 0)


def half(x, bit):
    middle = x.shape[-1] // 2
    return jnp.where(bit == 0, x[..., :middle], x[..., middle:])


def join(mine, other, bit, dim):
    low, high = jnp.where(bit == 0, mine, other), jnp.where(bit == 0, other, mine)
    return jnp.concatenate([low, high], dim)


def final_kernel(ceiling, place_ref, anchor_ref, own_ref, mine_ref, other_ref, *refs):
    pieces, sums, (out_ref, moment_ref, grad) = refs[:8], refs[8:16], refs[16:]
    step = pl.program_id(0)
    high = pieces[0].shape[0]
    row = sums[0][0:1, :]
    for part in sums[1:]:
        row = row + part[0:1, :]
    scaling = ceiling / jnp.maximum(jnp.sqrt(jnp.sum(row, axis=1, keepdims=True)), ceiling)
    factor = (outer_rate * (1.0 + momentum_decay)) * scaling
    swapped = place_ref[8] != 0
    parts = []
    for g in range(mine_ref.shape[0]):
        mine, other = mine_ref[g], other_ref[g]
        parts += [jnp.where(swapped, other, mine), jnp.where(swapped, mine, other)]
    moment = jnp.concatenate(parts, 0).T
    for i, piece in enumerate(pieces):
        at = pl.multiple_of(place_ref[i] * high, high)
        grad[pl.ds(at, high), :] = piece[...]
    rest = anchor_ref[...] - (outer_rate * momentum_decay * momentum_decay) * moment
    out_ref[...] = rest - factor * grad[...]

    @pl.when(step == place_ref[9])
    def _():
        shard = own_ref.shape[0]
        turned = grad[...].T
        own = turned[0:shard]
        for k in range(1, turned.shape[0] // shard):
            own = jnp.where(place_ref[10] == k, turned[k * shard : (k + 1) * shard], own)
        moment_ref[...] = momentum_decay * own_ref[...] + scaling * own


def final(ceiling, place, anchor, own_moment, mine, other, pieces):
    rows, cols = anchor.shape
    groups, shard, _ = mine.shape
    high = pieces[0].shape[0]
    per = 4
    width = per * 2 * shard
    block = pl.BlockSpec((rows, width), lambda i, p: (0, i))
    part = pl.BlockSpec((per, shard, rows), lambda i, p: (i, 0, 0))
    piece = pl.BlockSpec((high, width), lambda i, p: (0, i))
    squares = pl.BlockSpec((SUB, LANE), lambda i, p: (0, cols // LANE))
    whole = pl.BlockSpec(own_moment.shape, lambda i, p: (0, 0))
    count = len(pieces)
    return pl.pallas_call(
        lambda *refs: final_kernel(ceiling, *refs),
        out_shape=(
            jax.ShapeDtypeStruct(anchor.shape, anchor.dtype),
            jax.ShapeDtypeStruct(own_moment.shape, own_moment.dtype),
        ),
        grid_spec=pltpu.PrefetchScalarGridSpec(
            num_scalar_prefetch=1,
            grid=(groups // per,),
            in_specs=[block, whole, part, part] + [piece] * count + [squares] * count,
            out_specs=(block, whole),
            scratch_shapes=[pltpu.VMEM((rows, width), jnp.float32)],
        ),
        cost_estimate=pl.CostEstimate(flops=5 * rows * cols, bytes_accessed=16 * rows * cols, transcendentals=0),
        compiler_params=pltpu.CompilerParams(vmem_limit_bytes=56 << 20),
        name="final",
    )(place, anchor, own_moment, mine, other, *pieces, *pieces)


def on_device(anchor, local_weights, momentum):
    y, zh, core = (lax.axis_index(a) for a in REPLICA)
    replicas = math.prod(lax.axis_size(a) for a in REPLICA)
    elements = anchor.shape[0] * anchor.shape[1] * lax.axis_size("zl") * lax.axis_size("x")
    ceiling = clip_rms * math.sqrt(elements)
    rows, cols = anchor.shape
    blocks = rows // SUB
    a_rows = anchor.reshape(blocks, SUB, cols)
    l_rows = local_weights.reshape(blocks, SUB, cols)
    own_moment = momentum[:, 0, :].T
    shard = own_moment.shape[0]

    high = blocks // 8

    def drift(start, count):
        return rows_at(a_rows, start, count) - rows_at(l_rows, start, count)

    over_core = {}
    for pair in ((y >> 1) ^ 1, y >> 1):
        start = ((1 - core) * 4 + pair * 2) * high
        over_core[len(over_core)] = swap(drift(start, 2 * high), core=1)

    def summed(mask):
        at = rows_at(over_core[1 - (mask >> 1)], ((y ^ mask) & 1) * high, high)
        return drift((core * 4 + (y ^ mask)) * high, high) + at

    over_y = {}
    for mask in (3, 2, 1):
        over_y[mask] = swap(summed(mask), y=mask)
    moments = {0: own_moment}
    for mask in MASKS:
        moments[mask] = swap(own_moment, zh=mask)
    total = summed(0)
    for mask in (3, 2, 1):
        total = total + over_y[mask]

    def part_of(x, index):
        return half(rows_at(x, index >> 1, 1), index & 1)

    sends = {mask: part_of(total, zh ^ mask) for mask in MASKS}
    own = part_of(total, zh)

    moment = jnp.zeros((4, shard // SUB, SUB, LANE), own_moment.dtype)
    for mask, part in moments.items():
        part = after(part.reshape(shard // SUB, SUB, LANE), total)
        moment = lax.dynamic_update_index_in_dim(moment, part, zh ^ mask, 0)
    moment_y = hold(moment, sends[2])
    moments = {mask: swap(moment_y, y=mask) for mask in (1, 3)}
    for mask in MASKS:
        own = own + swap(sends[mask], zh=mask)
    own = own * (1.0 / replicas)
    moments[2] = swap(hold(moment, own), y=2)

    place = [(core ^ c) * 4 + (y ^ mask) for c in (0, 1) for mask in (0, 1, 3, 2)]
    place = jnp.stack(place + [core, (y * 8 + zh * 2 + core) // 8, zh * 2 + core]).astype(jnp.int32)

    def add_squares(squares, axes):
        n = math.prod(lax.axis_size(a) for a in axes)
        row = jnp.sum(squares, axis=0, keepdims=True)
        return jnp.sum(lax.all_to_all(jnp.broadcast_to(row, (n,) + row.shape), axes, 0, 0), axis=0)

    squares = jnp.sum(own.reshape(SUB, -1, LANE) ** 2, axis=1)
    back = {mask: swap(own, zh=mask) for mask in MASKS}
    squares = add_squares(squares, ("zh", "zl", "x"))
    own = join(join(own, back[1], zh & 1, 2), join(back[2], back[3], zh & 1, 2), zh >> 1, 0)

    squares = jnp.broadcast_to(squares, own.shape[:2] + (LANE,))
    squares = after(after(squares, moments[1]), moments[3])
    whole = jnp.zeros((4,) + moment.shape, own_moment.dtype)
    for mask, part in ((0, moment),) + tuple(moments.items()):
        whole = lax.dynamic_update_index_in_dim(whole, after(part, own), y ^ mask, 0)
    whole = whole.reshape(16, shard, LANE)
    own = jnp.concatenate([own, squares], 2)
    pieces = [own] + [swap(own, y=mask) for mask in (1, 3, 2)]
    pieces += [swap(piece, core=1) for piece in pieces]
    pieces = [piece.reshape(high * SUB, cols + LANE) for piece in pieces]
    new_anchor, new_moment = final(ceiling, place, anchor, own_moment, whole, swap(whole, core=1), pieces)
    return new_anchor, new_moment.T[:, None, :]


def solution(mesh):
    fine = Mesh(mesh.devices.reshape(4, 4, 2, 2, 4), ("y", "zh", "core", "zl", "x"))
    in_specs = (P("zl", "x"), P(REPLICA, "zl", "x"), P("zl", "x", REPLICA))
    out_specs = (P("zl", "x"), P("zl", "x", REPLICA))
    return jax.shard_map(on_device, mesh=fine, in_specs=in_specs, out_specs=out_specs, check_vma=False)
```

```python
import math

import jax
import jax.numpy as jnp
from jax import lax
from jax.experimental import pallas as pl
from jax.experimental.pallas import tpu as pltpu
from jax.sharding import Mesh, PartitionSpec as P

momentum_decay = 0.9
outer_rate = 0.7
clip_rms = 0.25

REPLICA = ("y", "zh", "core")
SUB = 8
LANE = 128
MASKS = (1, 3, 2)
HOLD_BYTES = 2 << 20
IN_VMEM = pl.BlockSpec(memory_space=pltpu.VMEM)


def swap(x, /, **masks):
    axes = tuple(masks)
    sizes = [lax.axis_size(a) for a in axes]
    mask = 0
    for a, n in zip(axes, sizes):
        mask = mask * n + masks[a]
    return lax.ppermute(x, axes, [(i, i ^ mask) for i in range(math.prod(sizes))])


def after(x, other):
    tile = other.reshape(-1, SUB, other.shape[-1])[0, :, :LANE]
    return x + 0.0 * jnp.clip(tile, -1.0, 1.0)


def hold_kernel(tile_ref, x_ref, out_ref):
    del tile_ref
    out_ref[...] = x_ref[...]


def hold(x, other):
    tile = other.reshape(-1, SUB, other.shape[-1])[0, :, :LANE]
    flat = x.reshape(-1, LANE)
    return pl.pallas_call(
        hold_kernel,
        out_shape=jax.ShapeDtypeStruct(flat.shape, flat.dtype),
        in_specs=[IN_VMEM, IN_VMEM],
        out_specs=IN_VMEM,
        cost_estimate=pl.CostEstimate(flops=0, bytes_accessed=HOLD_BYTES, transcendentals=0),
        compiler_params=pltpu.CompilerParams(vmem_limit_bytes=16 << 20),
        name="hold",
    )(tile, flat).reshape(x.shape)


def rows_at(x, start, count):
    return lax.dynamic_slice_in_dim(x, start, count, 0)


def half(x, bit):
    middle = x.shape[-1] // 2
    return jnp.where(bit == 0, x[..., :middle], x[..., middle:])


def join(mine, other, bit, dim):
    low, high = jnp.where(bit == 0, mine, other), jnp.where(bit == 0, other, mine)
    return jnp.concatenate([low, high], dim)


def final_kernel(ceiling, place_ref, anchor_ref, own_ref, mine_ref, other_ref, *refs):
    pieces, sums, (out_ref, moment_ref, grad) = refs[:8], refs[8:16], refs[16:]
    step = pl.program_id(0)
    high = pieces[0].shape[0]
    rows = [part[0:1, :] for part in sums]
    while len(rows) > 1:
        rows = [a + b for a, b in zip(rows[::2], rows[1::2])]
    scaling = ceiling / jnp.maximum(jnp.sqrt(jnp.sum(rows[0], axis=1, keepdims=True)), ceiling)
    factor = (outer_rate * (1.0 + momentum_decay)) * scaling
    swapped = place_ref[8] != 0
    parts = []
    for g in range(mine_ref.shape[0]):
        mine, other = mine_ref[g], other_ref[g]
        parts += [jnp.where(swapped, other, mine), jnp.where(swapped, mine, other)]
    moment = jnp.concatenate(parts, 0).T
    for i, piece in enumerate(pieces):
        at = pl.multiple_of(place_ref[i] * high, high)
        grad[pl.ds(at, high), :] = piece[...]
    rest = anchor_ref[...] - (outer_rate * momentum_decay * momentum_decay) * moment
    out_ref[...] = rest - factor * grad[...]

    @pl.when(step == place_ref[9])
    def _():
        shard = own_ref.shape[0]
        turned = grad[...].T
        own = turned[0:shard]
        for k in range(1, turned.shape[0] // shard):
            own = jnp.where(place_ref[10] == k, turned[k * shard : (k + 1) * shard], own)
        moment_ref[...] = momentum_decay * own_ref[...] + scaling * own


def final(ceiling, place, anchor, own_moment, mine, other, pieces):
    rows, cols = anchor.shape
    groups, shard, _ = mine.shape
    high = pieces[0].shape[0]
    per = 4
    width = per * 2 * shard
    block = pl.BlockSpec((rows, width), lambda i, p: (0, i))
    part = pl.BlockSpec((per, shard, rows), lambda i, p: (i, 0, 0))
    piece = pl.BlockSpec((high, width), lambda i, p: (0, i))
    squares = pl.BlockSpec((SUB, LANE), lambda i, p: (0, cols // LANE))
    whole = pl.BlockSpec(own_moment.shape, lambda i, p: (0, 0))
    count = len(pieces)
    return pl.pallas_call(
        lambda *refs: final_kernel(ceiling, *refs),
        out_shape=(
            jax.ShapeDtypeStruct(anchor.shape, anchor.dtype),
            jax.ShapeDtypeStruct(own_moment.shape, own_moment.dtype),
        ),
        grid_spec=pltpu.PrefetchScalarGridSpec(
            num_scalar_prefetch=1,
            grid=(groups // per,),
            in_specs=[block, whole, part, part] + [piece] * count + [squares] * count,
            out_specs=(block, whole),
            scratch_shapes=[pltpu.VMEM((rows, width), jnp.float32)],
        ),
        cost_estimate=pl.CostEstimate(flops=5 * rows * cols, bytes_accessed=16 * rows * cols, transcendentals=0),
        compiler_params=pltpu.CompilerParams(vmem_limit_bytes=56 << 20),
        name="final",
    )(place, anchor, own_moment, mine, other, *pieces, *pieces)


def on_device(anchor, local_weights, momentum):
    y, zh, core = (lax.axis_index(a) for a in REPLICA)
    replicas = math.prod(lax.axis_size(a) for a in REPLICA)
    elements = anchor.shape[0] * anchor.shape[1] * lax.axis_size("zl") * lax.axis_size("x")
    ceiling = clip_rms * math.sqrt(elements)
    rows, cols = anchor.shape
    blocks = rows // SUB
    a_rows = anchor.reshape(blocks, SUB, cols)
    l_rows = local_weights.reshape(blocks, SUB, cols)
    own_moment = momentum[:, 0, :].T
    shard = own_moment.shape[0]

    high = blocks // 8

    def drift(start, count):
        return rows_at(a_rows, start, count) - rows_at(l_rows, start, count)

    over_core = {}
    for pair in ((y >> 1) ^ 1, y >> 1):
        start = ((1 - core) * 4 + pair * 2) * high
        over_core[len(over_core)] = swap(drift(start, 2 * high), core=1)

    def summed(mask):
        at = rows_at(over_core[1 - (mask >> 1)], ((y ^ mask) & 1) * high, high)
        return drift((core * 4 + (y ^ mask)) * high, high) + at

    over_y = {}
    for mask in (3, 2, 1):
        over_y[mask] = swap(summed(mask), y=mask)
    moments = {0: own_moment}
    for mask in MASKS:
        moments[mask] = swap(own_moment, zh=mask)
    total = summed(0)
    for mask in (3, 2, 1):
        total = total + over_y[mask]

    def part_of(x, index):
        return half(rows_at(x, index >> 1, 1), index & 1)

    sends = {mask: part_of(total, zh ^ mask) for mask in MASKS}
    own = part_of(total, zh)

    moment = jnp.zeros((4, shard // SUB, SUB, LANE), own_moment.dtype)
    for mask, part in moments.items():
        part = after(part.reshape(shard // SUB, SUB, LANE), total)
        moment = lax.dynamic_update_index_in_dim(moment, part, zh ^ mask, 0)
    moment_y = hold(moment, sends[2])
    moments = {mask: swap(moment_y, y=mask) for mask in (1, 3)}
    for mask in MASKS:
        own = own + swap(sends[mask], zh=mask)
    own = own * (1.0 / replicas)
    moments[2] = swap(hold(moment, own), y=2)

    place = [(core ^ c) * 4 + (y ^ mask) for c in (0, 1) for mask in (0, 1, 3, 2)]
    place = jnp.stack(place + [core, (y * 8 + zh * 2 + core) // 8, zh * 2 + core]).astype(jnp.int32)

    def add_squares(squares, axes):
        n = math.prod(lax.axis_size(a) for a in axes)
        row = jnp.sum(squares, axis=0, keepdims=True)
        return jnp.sum(lax.all_to_all(jnp.broadcast_to(row, (n,) + row.shape), axes, 0, 0), axis=0)

    squares = jnp.sum(own.reshape(SUB, -1, LANE) ** 2, axis=1)
    back = {mask: swap(own, zh=mask) for mask in MASKS}
    squares = add_squares(squares, ("zh", "zl", "x"))
    own = join(join(own, back[1], zh & 1, 2), join(back[2], back[3], zh & 1, 2), zh >> 1, 0)

    squares = jnp.broadcast_to(squares, own.shape[:2] + (LANE,))
    squares = after(after(squares, moments[1]), moments[3])
    whole = jnp.zeros((4,) + moment.shape, own_moment.dtype)
    for mask, part in ((0, moment),) + tuple(moments.items()):
        whole = lax.dynamic_update_index_in_dim(whole, after(part, own), y ^ mask, 0)
    whole = whole.reshape(16, shard, LANE)
    own = jnp.concatenate([own, squares], 2)
    pieces = [own] + [swap(own, y=mask) for mask in (1, 3, 2)]
    pieces += [swap(piece, core=1) for piece in pieces]
    pieces = [piece.reshape(high * SUB, cols + LANE) for piece in pieces]
    new_anchor, new_moment = final(ceiling, place, anchor, own_moment, whole, swap(whole, core=1), pieces)
    return new_anchor, new_moment.T[:, None, :]


def solution(mesh):
    fine = Mesh(mesh.devices.reshape(4, 4, 2, 2, 4), ("y", "zh", "core", "zl", "x"))
    in_specs = (P("zl", "x"), P(REPLICA, "zl", "x"), P("zl", "x", REPLICA))
    out_specs = (P("zl", "x"), P("zl", "x", REPLICA))
    return jax.shard_map(on_device, mesh=fine, in_specs=in_specs, out_specs=out_specs, check_vma=False)
```

```python
import math

import jax
import jax.numpy as jnp
from jax import lax
from jax.experimental import pallas as pl
from jax.experimental.pallas import tpu as pltpu
from jax.sharding import Mesh, PartitionSpec as P

momentum_decay = 0.9
outer_rate = 0.7
clip_rms = 0.25

REPLICA = ("y", "zh", "core")
SUB = 8
LANE = 128
MASKS = (1, 3, 2)
HOLD_BYTES = 2 << 20
IN_VMEM = pl.BlockSpec(memory_space=pltpu.VMEM)


def swap(x, /, **masks):
    axes = tuple(masks)
    sizes = [lax.axis_size(a) for a in axes]
    mask = 0
    for a, n in zip(axes, sizes):
        mask = mask * n + masks[a]
    return lax.ppermute(x, axes, [(i, i ^ mask) for i in range(math.prod(sizes))])


def after(x, other):
    tile = other.reshape(-1, SUB, other.shape[-1])[0, :, :LANE]
    return x + 0.0 * jnp.clip(tile, -1.0, 1.0)


def hold_kernel(tile_ref, x_ref, out_ref):
    del tile_ref
    out_ref[...] = x_ref[...]


def hold(x, other):
    tile = other.reshape(-1, SUB, other.shape[-1])[0, :, :LANE]
    flat = x.reshape(-1, LANE)
    return pl.pallas_call(
        hold_kernel,
        out_shape=jax.ShapeDtypeStruct(flat.shape, flat.dtype),
        in_specs=[IN_VMEM, IN_VMEM],
        out_specs=IN_VMEM,
        cost_estimate=pl.CostEstimate(flops=0, bytes_accessed=HOLD_BYTES, transcendentals=0),
        compiler_params=pltpu.CompilerParams(vmem_limit_bytes=16 << 20),
        name="hold",
    )(tile, flat).reshape(x.shape)


def rows_at(x, start, count):
    return lax.dynamic_slice_in_dim(x, start, count, 0)


def half(x, bit):
    middle = x.shape[-1] // 2
    return jnp.where(bit == 0, x[..., :middle], x[..., middle:])


def join(mine, other, bit, dim):
    low, high = jnp.where(bit == 0, mine, other), jnp.where(bit == 0, other, mine)
    return jnp.concatenate([low, high], dim)


def final_kernel(ceiling, place_ref, anchor_ref, own_ref, mine_ref, other_ref, *refs):
    pieces, sums, (out_ref, moment_ref, grad) = refs[:8], refs[8:16], refs[16:]
    step = pl.program_id(0)
    high = pieces[0].shape[0]
    rows = [part[0:1, :] for part in sums]
    while len(rows) > 1:
        rows = [a + b for a, b in zip(rows[::2], rows[1::2])]
    scaling = ceiling / jnp.maximum(jnp.sqrt(jnp.sum(rows[0], axis=1, keepdims=True)), ceiling)
    factor = (outer_rate * (1.0 + momentum_decay)) * scaling
    swapped = place_ref[8] != 0
    parts = []
    for g in range(mine_ref.shape[0]):
        mine, other = mine_ref[g], other_ref[g]
        parts += [jnp.where(swapped, other, mine), jnp.where(swapped, mine, other)]
    moment = jnp.concatenate(parts, 0).T
    for i, piece in enumerate(pieces):
        at = pl.multiple_of(place_ref[i] * high, high)
        grad[pl.ds(at, high), :] = piece[...]
    rest = anchor_ref[...] - (outer_rate * momentum_decay * momentum_decay) * moment
    out_ref[...] = rest - factor * grad[...]

    @pl.when(step == place_ref[9])
    def _():
        shard = own_ref.shape[0]
        turned = grad[...].T
        own = turned[0:shard]
        for k in range(1, turned.shape[0] // shard):
            own = jnp.where(place_ref[10] == k, turned[k * shard : (k + 1) * shard], own)
        moment_ref[...] = momentum_decay * own_ref[...] + scaling * own


def final(ceiling, place, anchor, own_moment, mine, other, pieces):
    rows, cols = anchor.shape
    groups, shard, _ = mine.shape
    high = pieces[0].shape[0]
    per = 4
    width = per * 2 * shard
    block = pl.BlockSpec((rows, width), lambda i, p: (0, i))
    part = pl.BlockSpec((per, shard, rows), lambda i, p: (i, 0, 0))
    piece = pl.BlockSpec((high, width), lambda i, p: (0, i))
    squares = pl.BlockSpec((SUB, LANE), lambda i, p: (0, cols // LANE))
    whole = pl.BlockSpec(own_moment.shape, lambda i, p: (0, 0))
    count = len(pieces)
    return pl.pallas_call(
        lambda *refs: final_kernel(ceiling, *refs),
        out_shape=(
            jax.ShapeDtypeStruct(anchor.shape, anchor.dtype),
            jax.ShapeDtypeStruct(own_moment.shape, own_moment.dtype),
        ),
        grid_spec=pltpu.PrefetchScalarGridSpec(
            num_scalar_prefetch=1,
            grid=(groups // per,),
            in_specs=[block, whole, part, part] + [piece] * count + [squares] * count,
            out_specs=(block, whole),
            scratch_shapes=[pltpu.VMEM((rows, width), jnp.float32)],
        ),
        cost_estimate=pl.CostEstimate(flops=5 * rows * cols, bytes_accessed=16 * rows * cols, transcendentals=0),
        compiler_params=pltpu.CompilerParams(vmem_limit_bytes=56 << 20),
        name="final",
    )(place, anchor, own_moment, mine, other, *pieces, *pieces)


def on_device(anchor, local_weights, momentum):
    y, zh, core = (lax.axis_index(a) for a in REPLICA)
    replicas = math.prod(lax.axis_size(a) for a in REPLICA)
    elements = anchor.shape[0] * anchor.shape[1] * lax.axis_size("zl") * lax.axis_size("x")
    ceiling = clip_rms * math.sqrt(elements)
    rows, cols = anchor.shape
    blocks = rows // SUB
    a_rows = anchor.reshape(blocks, SUB, cols)
    l_rows = local_weights.reshape(blocks, SUB, cols)
    own_moment = momentum[:, 0, :].T
    shard = own_moment.shape[0]

    high = blocks // 8

    def drift(start, count):
        return rows_at(a_rows, start, count) - rows_at(l_rows, start, count)

    over_core = {}
    for pair in ((y >> 1) ^ 1, y >> 1):
        start = ((1 - core) * 4 + pair * 2) * high
        over_core[len(over_core)] = swap(drift(start, 2 * high), core=1)

    def summed(mask):
        at = rows_at(over_core[1 - (mask >> 1)], ((y ^ mask) & 1) * high, high)
        return drift((core * 4 + (y ^ mask)) * high, high) + at

    over_y = {}
    for mask in (3, 2, 1):
        over_y[mask] = swap(summed(mask), y=mask)
    moments = {0: own_moment}
    for mask in (2, 3, 1):
        moments[mask] = swap(own_moment, zh=mask)
    total = summed(0)
    for mask in (3, 2, 1):
        total = total + over_y[mask]

    def part_of(x, index):
        return half(rows_at(x, index >> 1, 1), index & 1)

    sends = {mask: part_of(total, zh ^ mask) for mask in MASKS}
    own = part_of(total, zh)

    moment = jnp.zeros((4, shard // SUB, SUB, LANE), own_moment.dtype)
    for mask, part in moments.items():
        part = after(part.reshape(shard // SUB, SUB, LANE), total)
        moment = lax.dynamic_update_index_in_dim(moment, part, zh ^ mask, 0)
    moment_y = hold(moment, sends[2])
    moments = {mask: swap(moment_y, y=mask) for mask in (1, 3)}
    for mask in MASKS:
        own = own + swap(sends[mask], zh=mask)
    own = own * (1.0 / replicas)
    moments[2] = swap(hold(moment, own), y=2)

    place = [(core ^ c) * 4 + (y ^ mask) for c in (0, 1) for mask in (0, 1, 3, 2)]
    place = jnp.stack(place + [core, (y * 8 + zh * 2 + core) // 8, zh * 2 + core]).astype(jnp.int32)

    def add_squares(squares, axes):
        n = math.prod(lax.axis_size(a) for a in axes)
        row = jnp.sum(squares, axis=0, keepdims=True)
        return jnp.sum(lax.all_to_all(jnp.broadcast_to(row, (n,) + row.shape), axes, 0, 0), axis=0)

    squares = jnp.sum(own.reshape(SUB, -1, LANE) ** 2, axis=1)
    back = {mask: swap(own, zh=mask) for mask in MASKS}
    squares = add_squares(squares, ("zh", "zl", "x"))
    own = join(join(own, back[1], zh & 1, 2), join(back[2], back[3], zh & 1, 2), zh >> 1, 0)

    squares = jnp.broadcast_to(squares, own.shape[:2] + (LANE,))
    squares = after(after(squares, moments[1]), moments[3])
    whole = jnp.zeros((4,) + moment.shape, own_moment.dtype)
    for mask, part in ((0, moment),) + tuple(moments.items()):
        whole = lax.dynamic_update_index_in_dim(whole, after(part, own), y ^ mask, 0)
    whole = whole.reshape(16, shard, LANE)
    own = jnp.concatenate([own, squares], 2)
    pieces = [own] + [swap(own, y=mask) for mask in (1, 3, 2)]
    pieces += [swap(piece, core=1) for piece in pieces]
    pieces = [piece.reshape(high * SUB, cols + LANE) for piece in pieces]
    new_anchor, new_moment = final(ceiling, place, anchor, own_moment, whole, swap(whole, core=1), pieces)
    return new_anchor, new_moment.T[:, None, :]


def solution(mesh):
    fine = Mesh(mesh.devices.reshape(4, 4, 2, 2, 4), ("y", "zh", "core", "zl", "x"))
    in_specs = (P("zl", "x"), P(REPLICA, "zl", "x"), P("zl", "x", REPLICA))
    out_specs = (P("zl", "x"), P("zl", "x", REPLICA))
    return jax.shard_map(on_device, mesh=fine, in_specs=in_specs, out_specs=out_specs, check_vma=False)
```
